32 devices in a mesh: seq: 8 (over y, x, core), batch: 4 (over z).
Axes of the slice: x: 2, y: 2, z: 4, core: 2. Of those that a mesh axis runs over, the one named last changes fastest.
Arguments:
- inputs: bfloat16 [32, 8192, 512], P('batch', 'seq'), may hold values from -32 to 32
- ln_gain: float32 [512], P(('seq', 'batch')), may hold values from 0.1 to 1.9
- ln_bias: float32 [512], P(('seq', 'batch')), may hold values from -3 to 3
- w_in: bfloat16 [512, 1024], P(('seq', 'batch')), may hold values from -0.25 to 0.25
- b_in: float32 [1024], P(('seq', 'batch')), may hold values from -3 to 3
- w_depth: float32 [512, 31], P(('seq', 'batch')), may hold values from -1 to 1
- bn_gain: float32 [512], P(('seq', 'batch')), may hold values from 0.1 to 1.9
- bn_bias: float32 [512], P(('seq', 'batch')), may hold values from -3 to 3
- w_out: bfloat16 [512, 512], P(('seq', 'batch')), may hold values from -0.25 to 0.25
- b_out: float32 [512], P(('seq', 'batch')), may hold values from -3 to 3
Outputs:
- result: float32 [32, 8192, 512], P('batch', 'seq')
The draws below stay inside these ranges and needn't reach their ends.
All inputs are finite; a program needn't handle non-finite values.
Results may differ from the reference program's by a relative error of at most 0.0015.
Values may be sent and summed in bfloat16 or wider, within the bound.
No kernel may reach another device: no remote copies, remote signals or barrier semaphores. Data moves between devices by JAX's collectives and lax.ppermute only.
A program may use at most 192 MiB of HBM per device.

```python
import jax
import jax.numpy as jnp
from jax import lax

D = 512
KS = 31
SEQS = 32
LENGTH = 8192


def compose_frames(seg_table, raw_noise, seg_index):
    segment_part = jax.vmap(lambda rows, index_row: rows[index_row])(seg_table, seg_index)
    smooth_sum = raw_noise[:, 0:LENGTH]
    for lag_index in range(1, 8):
        smooth_sum = smooth_sum + raw_noise[:, lag_index:lag_index + LENGTH]
    return segment_part + 0.6 / jnp.sqrt(8.0) * smooth_sum + 0.45 * raw_noise[:, 7:7 + LENGTH]


def draw_inputs(key, part):
    key = jax.random.fold_in(key, 11)
    key_list = jax.random.split(key, 6)
    position = jnp.arange(LENGTH, dtype=jnp.float32) / LENGTH
    seq_weight = 1.0 + 2.0 * jnp.arange(SEQS, dtype=jnp.float32) / max(SEQS - 1, 1)
    offset = position[None, :, None] * seq_weight[:, None, None]
    direction = jnp.clip(jax.random.normal(key_list[2], (D,), jnp.float32), -3.0, 3.0)
    seg_frames = 160
    seg_count = LENGTH // seg_frames + 2
    seg_shift = jax.random.randint(key_list[4], (SEQS, 1), 0, seg_frames)
    seg_index = (jnp.arange(LENGTH, dtype=jnp.int32)[None, :] + seg_shift) // seg_frames
    seg_table = jnp.clip(jax.random.normal(key_list[5], (SEQS, seg_count, D), jnp.float32), -4.0, 4.0)
    raw_noise = jnp.clip(jax.random.normal(key_list[0], (SEQS, LENGTH + 7, D), jnp.float32), -4.0, 4.0)
    channel_scale = jnp.exp(jax.random.uniform(key_list[1], (D,), jnp.float32, jnp.log(0.3), jnp.log(3.0)))
    frames = compose_frames(seg_table, raw_noise, seg_index)
    values = frames * channel_scale + offset * direction
    return jnp.clip(values, -32.0, 32.0).astype(jnp.bfloat16)


def level_of(stream_key, dims, cuts, low, largest):
    factor_of, own = 1.0, jax.random.fold_in(stream_key, 6)
    for dim, parts in cuts:
        heights = jnp.exp(jax.random.uniform(jax.random.fold_in(own, dim), (parts,), jnp.float32, low / len(cuts), largest / len(cuts)))
        factor_of = factor_of * jnp.repeat(heights, dims[dim] // parts).reshape([-1 if axis == dim else 1 for axis in range(len(dims))])
    return factor_of


def normal_values(key, shape, scale, bound, cuts=(), kind=jnp.bfloat16):
    drawn = scale * jax.random.normal(key, shape, jnp.float32)
    if cuts:
        drawn = drawn * level_of(key, shape, cuts, -0.22, 0.18)
    return jnp.clip(drawn, -bound, bound).astype(kind)


def setup_inputs(seed: int = 0) -> dict:
    seeds = jax.random.split(jax.random.key(seed), 11)
    inputs = draw_inputs(jax.random.fold_in(seeds[10], 71), 0)
    ln_gain = jnp.clip(1.0 + 0.18 * jax.random.normal(seeds[1], (D,), jnp.float32), 0.1, 1.9)
    ln_bias = normal_values(seeds[2], (D,), 0.5, 3.0, ((0, 32),), jnp.float32)
    w_in = normal_values(seeds[3], (D, 2 * D), D ** -0.5, 0.25, ((0, 32),))
    b_in = normal_values(seeds[4], (2 * D,), 0.5, 3.0, ((0, 32),), jnp.float32)
    w_depth = normal_values(seeds[5], (D, KS), KS ** -0.5, 1.0, ((0, 32),), jnp.float32)
    bn_gain = jnp.clip(1.0 + 0.18 * jax.random.normal(seeds[6], (D,), jnp.float32), 0.1, 1.9)
    bn_bias = normal_values(seeds[7], (D,), 0.5, 3.0, ((0, 32),), jnp.float32)
    w_out = normal_values(seeds[8], (D, D), D ** -0.5, 0.25, ((0, 32),))
    b_out = normal_values(seeds[9], (D,), 0.5, 3.0, ((0, 32),), jnp.float32)
    return {"inputs": inputs, "ln_gain": ln_gain, "ln_bias": ln_bias, "w_in": w_in, "b_in": b_in, "w_depth": w_depth, "bn_gain": bn_gain, "bn_bias": bn_bias, "w_out": w_out, "b_out": b_out}


EPSILON = 1e-05

def layer_normed(rows, ln_gain, ln_bias):
    centre = lax.optimization_barrier(jnp.mean(rows, axis=-1, keepdims=True))
    spread = lax.optimization_barrier(jnp.mean((rows - centre) ** 2, axis=-1, keepdims=True))
    return ((rows - centre) * lax.rsqrt(spread + EPSILON) * ln_gain + ln_bias).astype(jnp.bfloat16)

def gated(normed, w_in, b_in):
    hidden = jnp.dot(normed, w_in, preferred_element_type=jnp.float32) + b_in
    half_cols = hidden.shape[-1] // 2
    return hidden[:, :half_cols] * jax.nn.sigmoid(hidden[:, half_cols:])

def depthwise(glu_rows, w_depth):
    half_width = (w_depth.shape[1] - 1) // 2
    padded = jnp.pad(glu_rows, ((half_width, half_width), (0, 0)))
    frame_total = glu_rows.shape[0]
    summed = jnp.zeros_like(glu_rows)
    for tap_index in range(w_depth.shape[1]):
        summed = summed + padded[tap_index:tap_index + frame_total] * w_depth[:, tap_index]
    return summed

def reference(inputs, ln_gain, ln_bias, w_in, b_in, w_depth, bn_gain, bn_bias, w_out, b_out):

    def front(sequence):
        normed = layer_normed(sequence.astype(jnp.float32), ln_gain, ln_bias)
        return depthwise(gated(normed, w_in, b_in), w_depth)
    conv_out = lax.map(front, inputs)
    count = SEQS * LENGTH
    mean_value = lax.optimization_barrier(jnp.sum(conv_out, axis=(0, 1))) / count

    def deviation(block):
        return lax.optimization_barrier(jnp.sum((block - mean_value) ** 2, axis=0))
    variance = lax.optimization_barrier(jnp.sum(lax.map(deviation, conv_out), axis=0)) / count
    scale_factor = bn_gain * lax.rsqrt(variance + EPSILON)

    def back(pair):
        block, sequence = pair
        normal_act = (block - mean_value) * scale_factor + bn_bias
        act_value = (normal_act * jax.nn.sigmoid(normal_act)).astype(jnp.bfloat16)
        projected = jnp.dot(act_value, w_out, preferred_element_type=jnp.float32)
        return projected + b_out + sequence.astype(jnp.float32)
    return lax.map(back, (conv_out, inputs))
```

```python
import functools

import jax
import jax.numpy as jnp
from jax import lax
from jax.experimental import pallas as pl
from jax.experimental.pallas import tpu as pltpu
from jax.sharding import PartitionSpec as P

EPSILON = 1e-05
F32 = jnp.float32
BF16 = jnp.bfloat16
HALO = 16
LANES = 128
VMEM_LIMIT = 60 * 1024 * 1024
SUB = 8
C_LN_GAIN, C_LN_BIAS, C_BN_GAIN, C_BN_BIAS, C_B_OUT, C_B_IN = 0, 1, 2, 3, 4, 5


def bit_stages(seq_size, batch_size):
    stages = []
    for axis, size, low in (("batch", batch_size, 0), ("seq", seq_size, 1)):
        at, top = low, size.bit_length() - 1
        while at < top:
            bits = min(2, top - at)
            stages.append((axis, at, bits))
            at += bits
    if seq_size > 1:
        stages.append(("seq", 0, 1))
    return stages


def gather_relative(block, stages):
    blocks = block[None]
    for axis, shift, bits in stages:
        size = lax.axis_size(axis)
        parts = [blocks]
        for m in range(1, 1 << bits):
            pairs = [(i, i ^ (m << shift)) for i in range(size)]
            parts.append(lax.ppermute(blocks, axis, pairs))
        blocks = jnp.concatenate(parts, axis=0)
    return blocks


def relative_place(seq_xor, batch_xor, stages):
    place, weight = 0, 1
    for axis, shift, bits in stages:
        word = seq_xor if axis == "seq" else batch_xor
        digit = (word >> shift) & ((1 << bits) - 1)
        place = place + digit * weight
        weight <<= bits
    return place


def prep_kernel(stages, seq_size, batch_size, rows, width, half, me_ref, g_ref, wt_ref, wo_ref, p_ref, pt_ref, bb_ref, w_scr):
    seq_me, batch_me = me_ref[0], me_ref[1]
    small = 2 * width
    for s in range(seq_size):
        for b in range(batch_size):
            d = s * batch_size + b
            at = relative_place(seq_me ^ s, batch_me ^ b, stages)
            lo = d * rows
            w_scr[lo : lo + rows, :] = g_ref[at, :, 0:small].astype(F32) * 0.5
            wo_ref[lo : lo + rows, :] = g_ref[at, :, small + LANES :]
            cell = g_ref[at, :, small : small + LANES].astype(F32)
            cell = cell + pltpu.roll(cell, LANES // 2, 1)
            p_ref[lo : lo + rows, :] = cell
            for h in range(2):
                col = cell[:, C_B_IN + h : C_B_IN + h + 1] * 0.5
                bb_ref[2 * lo + h * rows : 2 * lo + (h + 1) * rows, :] = jnp.broadcast_to(col, (rows, LANES))
    for j in range(0, small, 256):
        wt_ref[j : j + 256, :] = w_scr[:, j : j + 256].T.astype(BF16)
    pt_ref[...] = p_ref[...].T


def front_kernel(taps, flags_ref, x_hbm, left_hbm, right_hbm, wt_ref, bb_ref, p_ref, pt_ref, y_ref, st_ref,
                 x_scr, g_scr, y_scr, s_scr, q_scr, sems):
    seqs, frames, width = x_hbm.shape
    step = pl.program_id(0)
    blocks = frames // LANES
    chunk = y_ref.shape[1]
    ext = frames + 2 * HALO

    def copies(s):
        return (
            pltpu.make_async_copy(left_hbm.at[s], x_scr.at[s, pl.ds(0, HALO), :], sems.at[s, 0]),
            pltpu.make_async_copy(x_hbm.at[s], x_scr.at[s, pl.ds(HALO, frames), :], sems.at[s, 1]),
            pltpu.make_async_copy(right_hbm.at[s], x_scr.at[s, pl.ds(HALO + frames, HALO), :], sems.at[s, 2]),
        )

    @pl.when(step == 0)
    def _():
        for s in range(seqs):
            for c in copies(s):
                c.start()
        for s in range(seqs):
            for c in copies(s):
                c.wait()

    gain = pt_ref[C_LN_GAIN : C_LN_GAIN + 1, :]
    bias = pt_ref[C_LN_BIAS : C_LN_BIAS + 1, :]

    def normed(rows):
        rows = rows.astype(F32)
        centre = jnp.mean(rows, axis=-1, keepdims=True)
        rows = rows - centre
        spread = jnp.mean(rows * rows, axis=-1, keepdims=True)
        return (rows * lax.rsqrt(spread + EPSILON) * gain + bias).astype(BF16)

    def gated(rows):
        hid = lax.dot_general(wt_ref[...], rows, (((1,), (1,)), ((), ())), preferred_element_type=F32)
        n = hid.shape[1] // LANES
        add = jnp.concatenate([bb_ref[...]] * n, axis=1)
        hid = hid + add
        val = hid[:width]
        return val + val * jnp.tanh(hid[width:])

    @pl.when(step < blocks)
    def _():
        at = pl.multiple_of(step * LANES, LANES)
        edge = jnp.where(step == 0, HALO * flags_ref[0], 0)
        for s in range(0, seqs, 2):
            rows = jnp.concatenate([x_scr[s, pl.ds(at, LANES), :], x_scr[s + 1, pl.ds(at, LANES), :]], axis=0)
            glu = gated(normed(rows))
            lane = lax.broadcasted_iota(jnp.int32, (1, LANES), 1)
            keep = lane >= edge
            for h in range(2):
                g_scr[pl.ds(pl.multiple_of((step * seqs + s + h) * width, width), width), :] = jnp.where(
                    keep, glu[:, h * LANES : (h + 1) * LANES], 0.0
                )

    @pl.when(step == blocks)
    def _():
        tail = 2 * HALO
        rows = jnp.concatenate([x_scr[s, frames:ext, :] for s in range(seqs)], axis=0)
        glu = gated(normed(rows))
        lane = lax.broadcasted_iota(jnp.int32, (1, LANES), 1)
        keep = lane < tail - HALO * flags_ref[1]
        per = LANES // tail
        for s in range(seqs):
            part = glu[:, (s // per) * LANES : (s // per + 1) * LANES]
            move = (s % per) * tail
            if move:
                part = pltpu.roll(part, LANES - move, 1)
            to = (blocks * seqs + s) * width
            g_scr[to : to + width, :] = jnp.where(keep, part, 0.0)

    @pl.when(step > blocks)
    def _():
        base = (step - blocks - 1) * chunk
        lane = lax.broadcasted_iota(jnp.int32, (SUB, LANES), 1)
        row = lax.broadcasted_iota(jnp.int32, (SUB, LANES), 0)
        reach = 4

        def channel(local):
            c = base + local
            g = g_scr[pl.ds(c, seqs * (blocks + 1), stride=width), :]
            left = g[: seqs * blocks].astype(BF16)
            right = g[seqs:].astype(BF16)
            rows = jnp.concatenate([left, right], axis=1)
            tap = jnp.broadcast_to(p_ref[pl.ds(c, 1), :], (SUB, LANES))
            tap = jnp.where(lane >= LANES - taps, tap, 0.0)
            first = pltpu.roll(tap, 0, 1, stride=1, stride_axis=0)
            low, high = [], []
            for k in range(LANES // SUB):
                f = first if k == 0 else pltpu.roll(first, SUB * k, 1)
                if k < reach:
                    under = lane < row + SUB * k
                    low.append(jnp.where(under, f, 0.0))
                    high.append(jnp.where(under, 0.0, f))
                else:
                    low.append(f)
            zero = jnp.zeros((LANES - reach * SUB, LANES), F32)
            band = jnp.concatenate(low + high + [zero], axis=0).astype(BF16)
            y = jnp.dot(rows, band, preferred_element_type=F32)
            y_scr[pl.ds(local, seqs * blocks, stride=chunk), :] = y
            parts = y.reshape(blocks, seqs, LANES)
            s_scr[pl.ds(c, 1), :] = jnp.sum(jnp.sum(parts, axis=0), axis=0, keepdims=True)
            q_scr[pl.ds(c, 1), :] = jnp.sum(jnp.sum(parts * parts, axis=0), axis=0, keepdims=True)

        unroll = 8

        @pl.loop(0, chunk // unroll)
        def _(i):
            for u in range(unroll):
                channel(i * unroll + u)

        y_ref[...] = y_scr[...].reshape(y_ref.shape).astype(BF16)

    @pl.when(step == pl.num_programs(0) - 1)
    def _():
        total = jnp.sum(s_scr[...].T, axis=0, keepdims=True)
        square = jnp.sum(q_scr[...].T, axis=0, keepdims=True)
        both = jnp.concatenate([total, square], axis=0)
        st_ref[...] = jnp.broadcast_to(both[None], st_ref.shape)


def back_kernel(count, st_ref, p_ref, pt_ref, y_ref, x_ref, wo_ref, o_ref, scale_scr, shift_scr):
    width = wo_ref.shape[0]

    @pl.when(pl.program_id(0) == 0)
    def _():
        both = jnp.sum(st_ref[...], axis=0)
        mean = both[0:1] * (1.0 / count)
        var = jnp.maximum(both[1:2] * (1.0 / count) - mean * mean, 0.0)
        scale = pt_ref[C_BN_GAIN : C_BN_GAIN + 1, :] * lax.rsqrt(var + EPSILON)
        shift = pt_ref[C_BN_BIAS : C_BN_BIAS + 1, :] - mean * scale
        scale_scr[...] = jnp.broadcast_to(scale * 0.5, (LANES, width)).T
        shift_scr[...] = jnp.broadcast_to(shift * 0.5, (LANES, width)).T

    out_bias = pt_ref[C_B_OUT : C_B_OUT + 1, :]
    for s in range(y_ref.shape[0]):
        half = y_ref[s].astype(F32) * scale_scr[...] + shift_scr[...]
        act = (half + half * jnp.tanh(half)).astype(BF16)
        proj = lax.dot_general(act, wo_ref[...], (((0,), (0,)), ((), ())), preferred_element_type=F32)
        o_ref[s] = proj + out_bias + x_ref[s].astype(F32)


def shards(inputs, ln_gain, ln_bias, w_in, b_in, w_depth, bn_gain, bn_bias, w_out, b_out):
    seqs, frames, width = inputs.shape
    rows, taps = w_depth.shape
    seq_size, batch_size = lax.axis_size("seq"), lax.axis_size("batch")
    devices = seq_size * batch_size
    seq_me, batch_me = lax.axis_index("seq"), lax.axis_index("batch")
    half = LANES // 2
    stages = bit_stages(seq_size, batch_size)

    small = jnp.concatenate(
        [jnp.stack([ln_gain, ln_bias, bn_gain, bn_bias, b_out], axis=1),
         b_in.reshape(2, rows).T,
         jnp.zeros((rows, half - 7 - taps), F32),
         w_depth[:, ::-1]], axis=1)
    high = lax.reduce_precision(small, 8, 7)
    low = small - high
    packed = jnp.concatenate([w_in, high.astype(BF16), low.astype(BF16), w_out], axis=1)
    gathered = gather_relative(packed, stages)

    ends = seq_size - 1
    left = lax.ppermute(inputs[:, frames - HALO :], "seq", [(i, i + 1) for i in range(ends)])
    right = lax.ppermute(inputs[:, :HALO], "seq", [(i + 1, i) for i in range(ends)])

    me = jnp.stack([seq_me, batch_me]).astype(jnp.int32)
    if rows % 16:
        order = jnp.stack([relative_place(seq_me ^ (d // batch_size), batch_me ^ (d % batch_size), stages) for d in range(devices)])
        flat = jnp.take(gathered, order, axis=0)
        bias_cells = flat[:, :, 2 * width : 2 * width + LANES].astype(F32)
        bias_cells = (bias_cells[:, :, C_B_IN : C_B_IN + 2] + bias_cells[:, :, half + C_B_IN : half + C_B_IN + 2])
        flat = flat.reshape(1, width, -1)
        pieces = (1, 1)
        me = jnp.zeros((2,), jnp.int32)
    else:
        flat, pieces = gathered, (seq_size, batch_size)
    block_rows = width // (pieces[0] * pieces[1])
    wt, wo, p, pt, bb = pl.pallas_call(
        functools.partial(prep_kernel, stages if pieces[0] > 1 else [], *pieces, block_rows, width, half),
        out_shape=(
            jax.ShapeDtypeStruct((2 * width, width), BF16),
            jax.ShapeDtypeStruct((width, width), BF16),
            jax.ShapeDtypeStruct((width, LANES), F32),
            jax.ShapeDtypeStruct((LANES, width), F32),
            jax.ShapeDtypeStruct((2 * width, LANES), F32),
        ),
        in_specs=[pl.BlockSpec(memory_space=pltpu.SMEM), pl.BlockSpec(memory_space=pltpu.VMEM)],
        out_specs=[pl.BlockSpec(memory_space=pltpu.VMEM)] * 5,
        scratch_shapes=[pltpu.VMEM((width, 2 * width), F32)],
        compiler_params=pltpu.CompilerParams(vmem_limit_bytes=VMEM_LIMIT),
        name="prep",
    )(me, flat)
    if rows % 16:
        bb = jnp.broadcast_to(bias_cells.transpose(0, 2, 1).reshape(2 * width, 1) * 0.5, (2 * width, LANES))

    blocks = frames // LANES
    chunk = 32
    flags = jnp.stack([seq_me == 0, seq_me == ends]).astype(jnp.int32)
    steps = blocks + 1 + width // chunk
    y, st = pl.pallas_call(
        functools.partial(front_kernel, taps),
        grid=(steps,),
        out_shape=(
            jax.ShapeDtypeStruct((seqs * blocks, width, LANES), BF16),
            jax.ShapeDtypeStruct((devices, 2, width), F32),
        ),
        in_specs=[
            pl.BlockSpec(memory_space=pltpu.SMEM),
            pl.BlockSpec(memory_space=pl.ANY),
            pl.BlockSpec(memory_space=pl.ANY),
            pl.BlockSpec(memory_space=pl.ANY),
        ] + [pl.BlockSpec(memory_space=pltpu.VMEM)] * 4,
        out_specs=[
            pl.BlockSpec((seqs * blocks, chunk, LANES), lambda i: (0, jnp.maximum(i - blocks - 1, 0), 0)),
            pl.BlockSpec((devices, 2, width), lambda i: (0, 0, 0)),
        ],
        scratch_shapes=[
            pltpu.VMEM((seqs, frames + 2 * HALO, width), BF16),
            pltpu.VMEM(((blocks + 1) * seqs * width, LANES), F32),
            pltpu.VMEM((seqs * blocks * chunk, LANES), F32),
            pltpu.VMEM((width, LANES), F32),
            pltpu.VMEM((width, LANES), F32),
            pltpu.SemaphoreType.DMA((seqs, 3)),
        ],
        compiler_params=pltpu.CompilerParams(vmem_limit_bytes=VMEM_LIMIT),
        name="front",
    )(flags, inputs, left, right, wt, bb, p, pt)

    st = lax.all_to_all(st, ("seq", "batch"), 0, 0)

    count = float(seqs * frames * devices)
    group = 4
    per = seqs // group
    return pl.pallas_call(
        functools.partial(back_kernel, count),
        grid=(blocks * per,),
        out_shape=jax.ShapeDtypeStruct((seqs, frames, width), F32),
        in_specs=[
            pl.BlockSpec((devices, 2, width), lambda i: (0, 0, 0)),
            pl.BlockSpec((width, LANES), lambda i: (0, 0)),
            pl.BlockSpec((LANES, width), lambda i: (0, 0)),
            pl.BlockSpec((group, width, LANES), lambda i: (i, 0, 0)),
            pl.BlockSpec((group, LANES, width), lambda i: (i % per, i // per, 0)),
            pl.BlockSpec((width, width), lambda i: (0, 0)),
        ],
        out_specs=pl.BlockSpec((group, LANES, width), lambda i: (i % per, i // per, 0)),
        scratch_shapes=[pltpu.VMEM((width, LANES), F32), pltpu.VMEM((width, LANES), F32)],
        compiler_params=pltpu.CompilerParams(vmem_limit_bytes=VMEM_LIMIT),
        name="back",
    )(st, p, pt, y, inputs, wo)


def solution(mesh):
    channel = P(("seq", "batch"))
    matrix = P(("seq", "batch"), None)
    return jax.shard_map(
        shards,
        mesh=mesh,
        in_specs=(
            P("batch", "seq", None), channel, channel, matrix, channel, matrix, channel, channel, matrix, channel,
        ),
        out_specs=P("batch", "seq", None),
        check_vma=False,
    )
```

```python
import functools

import jax
import jax.numpy as jnp
from jax import lax
from jax.experimental import pallas as pl
from jax.experimental.pallas import tpu as pltpu
from jax.sharding import PartitionSpec as P

EPSILON = 1e-05
F32 = jnp.float32
BF16 = jnp.bfloat16
HALO = 16
LANES = 128
FRONT_VMEM = 36 * 1024 * 1024
BACK_VMEM = 16 * 1024 * 1024
SUB = 8
C_LN_GAIN, C_LN_BIAS, C_BN_GAIN, C_BN_BIAS, C_B_OUT, C_B_IN = 0, 1, 2, 3, 4, 5


def bit_stages(seq_size, batch_size):
    stages = []
    for axis, size, low in (("batch", batch_size, 0), ("seq", seq_size, 1)):
        at, top = low, size.bit_length() - 1
        while at < top:
            bits = min(2, top - at)
            stages.append((axis, at, bits))
            at += bits
    if seq_size > 1:
        stages.append(("seq", 0, 1))
    return stages


def gather_relative(block, stages):
    blocks = block[None]
    for axis, shift, bits in stages:
        size = lax.axis_size(axis)
        parts = [blocks]
        for m in range(1, 1 << bits):
            pairs = [(i, i ^ (m << shift)) for i in range(size)]
            parts.append(lax.ppermute(blocks, axis, pairs))
        blocks = jnp.concatenate(parts, axis=0)
    return blocks


def relative_place(seq_xor, batch_xor, stages):
    place, weight = 0, 1
    for axis, shift, bits in stages:
        word = seq_xor if axis == "seq" else batch_xor
        digit = (word >> shift) & ((1 << bits) - 1)
        place = place + digit * weight
        weight <<= bits
    return place


def pack_kernel(taps, ln_gain, ln_bias, w_in, b_in, w_depth, bn_gain, bn_bias, w_out, b_out, o_ref):
    rows, small = w_in.shape
    lane = lax.broadcasted_iota(jnp.int32, (rows, LANES), 1)
    row = lax.broadcasted_iota(jnp.int32, (rows, LANES), 0)

    def column(ref, start=0):
        line = jnp.broadcast_to(ref[...].reshape(1, -1), (rows, ref.shape[0]))
        hit = lane[:, : line.shape[1]] == row[:, : line.shape[1]] + start
        return jnp.sum(jnp.where(hit, line, 0.0), axis=1, keepdims=True)

    cells = (
        (C_LN_GAIN, column(ln_gain)),
        (C_LN_BIAS, column(ln_bias)),
        (C_BN_GAIN, column(bn_gain)),
        (C_BN_BIAS, column(bn_bias)),
        (C_B_OUT, column(b_out)),
        (C_B_IN, column(b_in)),
        (C_B_IN + 1, column(b_in, rows)),
    ) + tuple((LANES // 2 - 1 - k, w_depth[:, k : k + 1]) for k in range(taps))
    cell = jnp.zeros((rows, LANES), F32)
    for at, value in cells:
        cell = jnp.where((lane & (LANES // 2 - 1)) == at, value, cell)
    high = cell.astype(BF16)
    low = (cell - high.astype(F32)).astype(BF16)
    o_ref[:, :small] = w_in[...]
    o_ref[:, small : small + LANES] = jnp.where(lane < LANES // 2, high.astype(F32), low.astype(F32)).astype(BF16)
    o_ref[:, small + LANES :] = w_out[...]


def front_kernel(taps, stages, seq_size, batch_size, where_ref, flat_ref, x_ref, left_ref, right_ref,
                 y_ref, st_ref, wo_ref, pt_ref,
                 w_scr, wt_scr, bb_scr, p_scr, g_scr, y_scr, s_scr, q_scr):
    seqs, frames, width = x_ref.shape
    blocks = frames // LANES
    chunk = y_scr.shape[0] // (seqs * blocks)
    small = 2 * width
    rows = width // (seq_size * batch_size)
    seq_me, batch_me = where_ref[0], where_ref[1]
    first_edge, last_edge = where_ref[2], where_ref[3]

    for s in range(seq_size):
        for b in range(batch_size):
            lo = (s * batch_size + b) * rows
            at = relative_place(seq_me ^ s, batch_me ^ b, stages)
            w_scr[lo : lo + rows, :] = flat_ref[at, :, 0:small].astype(F32) * 0.5
            wo_ref[lo : lo + rows, :] = flat_ref[at, :, small + LANES :]
            cell = flat_ref[at, :, small : small + LANES].astype(F32)
            cell = cell + pltpu.roll(cell, LANES // 2, 1)
            p_scr[lo : lo + rows, :] = cell
            for h in range(2):
                col = cell[:, C_B_IN + h : C_B_IN + h + 1] * 0.5
                bb_scr[2 * lo + h * rows : 2 * lo + (h + 1) * rows, :] = jnp.broadcast_to(col, (rows, LANES))
    for j in range(0, small, 256):
        wt_scr[j : j + 256, :] = w_scr[:, j : j + 256].T.astype(BF16)
    pt_ref[...] = p_scr[...].T

    gain = pt_ref[C_LN_GAIN : C_LN_GAIN + 1, :]
    bias = pt_ref[C_LN_BIAS : C_LN_BIAS + 1, :]

    def normed(part):
        part = part.astype(F32)
        centre = jnp.mean(part, axis=-1, keepdims=True)
        part = part - centre
        spread = jnp.mean(part * part, axis=-1, keepdims=True)
        return (part * lax.rsqrt(spread + EPSILON) * gain + bias).astype(BF16)

    def gated(part):
        hid = lax.dot_general(wt_scr[...], part, (((1,), (1,)), ((), ())), preferred_element_type=F32)
        add = jnp.concatenate([bb_scr[...]] * (hid.shape[1] // LANES), axis=1)
        hid = hid + add
        val = hid[:width]
        return val + val * jnp.tanh(hid[width:])

    lane = lax.broadcasted_iota(jnp.int32, (1, LANES), 1)

    def block(b, piece, edge):
        for s in range(0, seqs, 2):
            glu = gated(normed(jnp.concatenate([piece(s), piece(s + 1)], axis=0)))
            for h in range(2):
                part = glu[:, h * LANES : (h + 1) * LANES]
                if edge is not None:
                    part = jnp.where(lane >= edge, part, 0.0)
                to = (b * seqs + s + h) * width
                g_scr[pl.ds(to if isinstance(b, int) else pl.multiple_of(to, width), width), :] = part

    block(0, lambda s: jnp.concatenate([left_ref[s], x_ref[s, : LANES - HALO, :]], axis=0), HALO * first_edge)

    @pl.loop(1, blocks)
    def _(b):
        at = pl.multiple_of(b * LANES - HALO, HALO)
        block(b, lambda s: x_ref[s, pl.ds(at, LANES), :], None)

    tail = 2 * HALO
    ends = []
    for s in range(seqs):
        ends += [x_ref[s, frames - HALO :, :], right_ref[s]]
    glu = gated(normed(jnp.concatenate(ends, axis=0)))
    per = LANES // tail
    for s in range(seqs):
        part = glu[:, (s // per) * LANES : (s // per + 1) * LANES]
        move = (s % per) * tail
        if move:
            part = pltpu.roll(part, LANES - move, 1)
        to = (blocks * seqs + s) * width
        g_scr[to : to + width, :] = jnp.where(lane < tail - HALO * last_edge, part, 0.0)

    wide = lax.broadcasted_iota(jnp.int32, (SUB, LANES), 1)
    row = lax.broadcasted_iota(jnp.int32, (SUB, LANES), 0)
    reach = 4

    def channel(c, local):
        g = g_scr[pl.ds(c, seqs * (blocks + 1), stride=width), :]
        pair = jnp.concatenate([g[: seqs * blocks].astype(BF16), g[seqs:].astype(BF16)], axis=1)
        tap = jnp.broadcast_to(p_scr[pl.ds(c, 1), :], (SUB, LANES))
        tap = jnp.where(wide >= LANES - taps, tap, 0.0)
        first = pltpu.roll(tap, 0, 1, stride=1, stride_axis=0)
        low, high = [], []
        for k in range(LANES // SUB):
            f = first if k == 0 else pltpu.roll(first, SUB * k, 1)
            if k < reach:
                under = wide < row + SUB * k
                low.append(jnp.where(under, f, 0.0))
                high.append(jnp.where(under, 0.0, f))
            else:
                low.append(f)
        zero = jnp.zeros((LANES - reach * SUB, LANES), F32)
        band = jnp.concatenate(low + high + [zero], axis=0).astype(BF16)
        y = jnp.dot(pair, band, preferred_element_type=F32)
        y_scr[pl.ds(local, seqs * blocks, stride=chunk), :] = y
        parts = y.reshape(blocks, seqs, LANES)
        s_scr[pl.ds(c, 1), :] = jnp.sum(jnp.sum(parts, axis=0), axis=0, keepdims=True)
        q_scr[pl.ds(c, 1), :] = jnp.sum(jnp.sum(parts * parts, axis=0), axis=0, keepdims=True)

    unroll = 16

    @pl.loop(0, width // chunk)
    def _(n):
        base = pl.multiple_of(n * chunk, chunk)

        @pl.loop(0, chunk // unroll)
        def _(i):
            for u in range(unroll):
                local = i * unroll + u
                channel(base + local, local)

        y_ref[:, pl.ds(base, chunk), :] = y_scr[...].reshape(seqs * blocks, chunk, LANES).astype(BF16)

    total = jnp.sum(s_scr[...].T, axis=0, keepdims=True)
    square = jnp.sum(q_scr[...].T, axis=0, keepdims=True)
    st_ref[...] = jnp.broadcast_to(jnp.concatenate([total, square], axis=0)[None], st_ref.shape)


def back_kernel(count, st_ref, pt_ref, y_ref, x_ref, wo_ref, o_hbm, scale_scr, shift_scr, o_scr, sems):
    seqs, frames, width = x_ref.shape
    blocks = frames // LANES
    group = o_scr.shape[1]
    per = seqs // group
    both = jnp.sum(st_ref[...], axis=0)
    mean = both[0:1] * (1.0 / count)
    var = jnp.maximum(both[1:2] * (1.0 / count) - mean * mean, 0.0)
    scale = pt_ref[C_BN_GAIN : C_BN_GAIN + 1, :] * lax.rsqrt(var + EPSILON)
    shift = pt_ref[C_BN_BIAS : C_BN_BIAS + 1, :] - mean * scale
    scale_scr[...] = jnp.broadcast_to(scale * 0.5, (LANES, width)).T
    shift_scr[...] = jnp.broadcast_to(shift * 0.5, (LANES, width)).T
    out_bias = pt_ref[C_B_OUT : C_B_OUT + 1, :]

    def copy(b, p):
        target = o_hbm.at[pl.ds(p * group, group), pl.ds(pl.multiple_of(b * LANES, LANES), LANES), :]
        return pltpu.make_async_copy(o_scr.at[p], target, sems.at[p])

    @pl.loop(0, blocks)
    def _(b):
        for p in range(per):
            acts = []
            for s in range(group):
                half = y_ref[b * seqs + p * group + s].astype(F32) * scale_scr[...] + shift_scr[...]
                acts.append((half + half * jnp.tanh(half)).astype(BF16))
            act = jnp.concatenate(acts, axis=1)
            proj = lax.dot_general(act, wo_ref[...], (((0,), (0,)), ((), ())), preferred_element_type=F32)

            @pl.when(b > 0)
            def _():
                copy(b - 1, p).wait()

            at = pl.multiple_of(b * LANES, LANES)
            for s in range(group):
                rest = x_ref[p * group + s, pl.ds(at, LANES), :].astype(F32) + out_bias
                o_scr[p, s] = proj[LANES * s : LANES * (s + 1)] + rest
            copy(b, p).start()

    for p in range(per):
        copy(blocks - 1, p).wait()


def shards(inputs, ln_gain, ln_bias, w_in, b_in, w_depth, bn_gain, bn_bias, w_out, b_out):
    seqs, frames, width = inputs.shape
    rows, taps = w_depth.shape
    seq_size, batch_size = lax.axis_size("seq"), lax.axis_size("batch")
    devices = seq_size * batch_size
    seq_me, batch_me = lax.axis_index("seq"), lax.axis_index("batch")
    stages = bit_stages(seq_size, batch_size)
    vmem = pl.BlockSpec(memory_space=pltpu.VMEM)
    blocks = frames // LANES

    packed = pl.pallas_call(
        functools.partial(pack_kernel, taps),
        out_shape=jax.ShapeDtypeStruct((rows, 3 * width + LANES), BF16),
        in_specs=[vmem] * 9,
        out_specs=vmem,
        name="pack",
    )(ln_gain, ln_bias, w_in, b_in, w_depth, bn_gain, bn_bias, w_out, b_out)
    ends = seq_size - 1
    left = lax.ppermute(inputs[:, frames - HALO :], "seq", [(i, i + 1) for i in range(ends)])
    right = lax.ppermute(inputs[:, :HALO], "seq", [(i + 1, i) for i in range(ends)])
    flat = gather_relative(packed, stages)

    pieces, at = (seq_size, batch_size), (seq_me, batch_me)
    if rows % 16:
        order = jnp.stack([relative_place(seq_me ^ (d // batch_size), batch_me ^ (d % batch_size), stages) for d in range(devices)])
        flat = jnp.take(flat, order, axis=0)
        for start in (2 * width + C_B_IN, 2 * width + LANES // 2 + C_B_IN):
            cut = flat[:, :, start : start + 2].transpose(0, 2, 1).reshape(2, width).T.reshape(devices, rows, 2)
            flat = lax.dynamic_update_slice(flat, cut, (0, 0, start))
        flat = flat.reshape(1, width, -1)
        pieces, at, stages = (1, 1), (0 * seq_me, 0 * batch_me), []
    place = jnp.stack([*at, seq_me == 0, seq_me == ends]).astype(jnp.int32)

    chunk = 64
    x = pltpu.with_memory_space_constraint(inputs, pltpu.VMEM)
    y, st, wo, pt = pl.pallas_call(
        functools.partial(front_kernel, taps, stages, *pieces),
        out_shape=(
            pltpu.VMEM((seqs * blocks, width, LANES), BF16),
            jax.ShapeDtypeStruct((devices, 2, width), F32),
            pltpu.VMEM((width, width), BF16),
            pltpu.VMEM((LANES, width), F32),
        ),
        in_specs=[pl.BlockSpec(memory_space=pltpu.SMEM)] + [vmem] * 4,
        out_specs=[vmem] * 4,
        scratch_shapes=[
            pltpu.VMEM((width, 2 * width), F32),
            pltpu.VMEM((2 * width, width), BF16),
            pltpu.VMEM((2 * width, LANES), F32),
            pltpu.VMEM((width, LANES), F32),
            pltpu.VMEM(((blocks + 1) * seqs * width, LANES), F32),
            pltpu.VMEM((seqs * blocks * chunk, LANES), F32),
            pltpu.VMEM((width, LANES), F32),
            pltpu.VMEM((width, LANES), F32),
        ],
        compiler_params=pltpu.CompilerParams(vmem_limit_bytes=FRONT_VMEM),
        name="front",
    )(place, flat, x, left, right)

    st = lax.all_to_all(st, ("seq", "batch"), 0, 0)

    group = 4
    y, x, wo, pt = (pltpu.with_memory_space_constraint(a, pltpu.VMEM) for a in (y, x, wo, pt))
    return pl.pallas_call(
        functools.partial(back_kernel, float(seqs * frames * devices)),
        out_shape=jax.ShapeDtypeStruct((seqs, frames, width), F32),
        in_specs=[vmem] * 5,
        out_specs=pl.BlockSpec(memory_space=pl.ANY),
        scratch_shapes=[
            pltpu.VMEM((width, LANES), F32),
            pltpu.VMEM((width, LANES), F32),
            pltpu.VMEM((seqs // group, group, LANES, width), F32),
            pltpu.SemaphoreType.DMA((seqs // group,)),
        ],
        compiler_params=pltpu.CompilerParams(vmem_limit_bytes=BACK_VMEM),
        name="back",
    )(st, pt, y, x, wo)


def solution(mesh):
    channel = P(("seq", "batch"))
    matrix = P(("seq", "batch"), None)
    return jax.shard_map(
        shards,
        mesh=mesh,
        in_specs=(
            P("batch", "seq", None), channel, channel, matrix, channel, matrix, channel, channel, matrix, channel,
        ),
        out_specs=P("batch", "seq", None),
        check_vma=False,
    )
```

```python
import functools

import jax
import jax.numpy as jnp
from jax import lax
from jax.experimental import pallas as pl
from jax.experimental.pallas import tpu as pltpu
from jax.sharding import PartitionSpec as P

EPSILON = 1e-05
F32 = jnp.float32
BF16 = jnp.bfloat16
HALO = 16
LANES = 128
FRONT_VMEM = 36 * 1024 * 1024
BACK_VMEM = 16 * 1024 * 1024
SUB = 8
C_LN_GAIN, C_LN_BIAS, C_BN_GAIN, C_BN_BIAS, C_B_OUT, C_B_IN = 0, 1, 2, 3, 4, 5


def bit_stages(seq_size, batch_size):
    stages = []
    for axis, size, low in (("batch", batch_size, 0), ("seq", seq_size, 1)):
        at, top = low, size.bit_length() - 1
        while at < top:
            bits = min(2, top - at)
            stages.append((axis, at, bits))
            at += bits
    if seq_size > 1:
        stages.append(("seq", 0, 1))
    return stages


def gather_relative(block, stages, keep):
    lists = [block[None]]
    for index, (axis, shift, bits) in enumerate(stages):
        if index <= len(stages) - keep:
            lists = [lists[0] if len(lists) == 1 else jnp.concatenate(lists, axis=0)]
        size = lax.axis_size(axis)
        parts = list(lists)
        for m in range(1, 1 << bits):
            pairs = [(i, i ^ (m << shift)) for i in range(size)]
            parts += [lax.ppermute(a, axis, pairs) for a in lists]
        lists = parts
    return lists


def relative_place(seq_xor, batch_xor, stages):
    place, weight = 0, 1
    for axis, shift, bits in stages:
        word = seq_xor if axis == "seq" else batch_xor
        digit = (word >> shift) & ((1 << bits) - 1)
        place = place + digit * weight
        weight <<= bits
    return place


def pack_kernel(taps, ln_gain, ln_bias, w_in, b_in, w_depth, bn_gain, bn_bias, w_out, b_out, o_ref):
    rows, small = w_in.shape
    lane = lax.broadcasted_iota(jnp.int32, (rows, LANES), 1)
    row = lax.broadcasted_iota(jnp.int32, (rows, LANES), 0)

    def column(ref, start=0):
        line = jnp.broadcast_to(ref[...].reshape(1, -1), (rows, ref.shape[0]))
        hit = lane[:, : line.shape[1]] == row[:, : line.shape[1]] + start
        return jnp.sum(jnp.where(hit, line, 0.0), axis=1, keepdims=True)

    cells = (
        (C_LN_GAIN, column(ln_gain)),
        (C_LN_BIAS, column(ln_bias)),
        (C_BN_GAIN, column(bn_gain)),
        (C_BN_BIAS, column(bn_bias)),
        (C_B_OUT, column(b_out)),
        (C_B_IN, column(b_in)),
        (C_B_IN + 1, column(b_in, rows)),
    ) + tuple((LANES // 2 - 1 - k, w_depth[:, k : k + 1]) for k in range(taps))
    cell = jnp.zeros((rows, LANES), F32)
    for at, value in cells:
        cell = jnp.where((lane & (LANES // 2 - 1)) == at, value, cell)
    high = cell.astype(BF16)
    low = (cell - high.astype(F32)).astype(BF16)
    o_ref[:, :small] = w_in[...]
    o_ref[:, small : small + LANES] = jnp.where(lane < LANES // 2, high.astype(F32), low.astype(F32)).astype(BF16)
    o_ref[:, small + LANES :] = w_out[...]


def front_kernel(taps, stages, seq_size, batch_size, where_ref, *refs):
    flat_refs, refs = refs[:-17], refs[-17:]
    front_body(taps, stages, seq_size, batch_size, where_ref, flat_refs, *refs)


def front_body(taps, stages, seq_size, batch_size, where_ref, flat_refs, x_hbm, left_ref, right_ref,
                 y_ref, st_ref, wo_ref, pt_ref, x_ref,
                 w_scr, wt_scr, bb_scr, p_scr, g_scr, y_scr, s_scr, q_scr, sems):
    seqs, frames, width = x_ref.shape
    blocks = frames // LANES
    chunk = y_scr.shape[0] // (seqs * blocks) - 1
    small = 2 * width
    rows = width // (seq_size * batch_size)
    seq_me, batch_me = where_ref[0], where_ref[1]
    first_edge, last_edge = where_ref[2], where_ref[3]

    loads = [pltpu.make_async_copy(x_hbm.at[s], x_ref.at[s], sems.at[s]) for s in range(seqs)]
    for load in loads:
        load.start()

    for s in range(seq_size):
        for b in range(batch_size):
            at = relative_place(s, b, stages)
            flat_ref, at = flat_refs[at // flat_refs[0].shape[0]], at % flat_refs[0].shape[0]
            lo = pl.multiple_of(((seq_me ^ s) * batch_size + (batch_me ^ b)) * rows, rows)
            w_scr[pl.ds(lo, rows), :] = flat_ref[at, :, 0:small].astype(F32) * 0.5
            wo_ref[pl.ds(lo, rows), :] = flat_ref[at, :, small + LANES :]
            cell = flat_ref[at, :, small : small + LANES].astype(F32)
            cell = cell + pltpu.roll(cell, LANES // 2, 1)
            p_scr[pl.ds(lo, rows), :] = cell
            for h in range(2):
                col = cell[:, C_B_IN + h : C_B_IN + h + 1] * 0.5
                bb_scr[pl.ds(pl.multiple_of(2 * lo + h * rows, rows), rows), :] = jnp.broadcast_to(col, (rows, LANES))
    for j in range(0, small, 256):
        wt_scr[j : j + 256, :] = w_scr[:, j : j + 256].T.astype(BF16)
    pt_ref[...] = p_scr[...].T
    for load in loads:
        load.wait()

    gain = pt_ref[C_LN_GAIN : C_LN_GAIN + 1, :]
    bias = pt_ref[C_LN_BIAS : C_LN_BIAS + 1, :]

    def normed(part):
        part = part.astype(F32)
        centre = jnp.mean(part, axis=-1, keepdims=True)
        part = part - centre
        spread = jnp.mean(part * part, axis=-1, keepdims=True)
        return (part * lax.rsqrt(spread + EPSILON) * gain + bias).astype(BF16)

    def gated(part):
        hid = lax.dot_general(wt_scr[...], part, (((1,), (1,)), ((), ())), preferred_element_type=F32)
        add = jnp.concatenate([bb_scr[...]] * (hid.shape[1] // LANES), axis=1)
        hid = hid + add
        val = hid[:width]
        return val + val * jnp.tanh(hid[width:])

    lane = lax.broadcasted_iota(jnp.int32, (1, LANES), 1)

    def block(b, piece, edge):
        for s in range(0, seqs, 2):
            glu = gated(normed(jnp.concatenate([piece(s), piece(s + 1)], axis=0)))
            for h in range(2):
                part = glu[:, h * LANES : (h + 1) * LANES]
                if edge is not None:
                    part = jnp.where(lane >= edge, part, 0.0)
                to = (b * seqs + s + h) * width
                g_scr[pl.ds(to if isinstance(b, int) else pl.multiple_of(to, width), width), :] = part

    block(0, lambda s: jnp.concatenate([left_ref[s], x_ref[s, : LANES - HALO, :]], axis=0), HALO * first_edge)

    @pl.loop(1, blocks)
    def _(b):
        at = pl.multiple_of(b * LANES - HALO, HALO)
        block(b, lambda s: x_ref[s, pl.ds(at, LANES), :], None)

    tail = 2 * HALO
    ends = []
    for s in range(seqs):
        ends += [x_ref[s, frames - HALO :, :], right_ref[s]]
    glu = gated(normed(jnp.concatenate(ends, axis=0)))
    per = LANES // tail
    for s in range(seqs):
        part = glu[:, (s // per) * LANES : (s // per + 1) * LANES]
        move = (s % per) * tail
        if move:
            part = pltpu.roll(part, LANES - move, 1)
        to = (blocks * seqs + s) * width
        g_scr[to : to + width, :] = jnp.where(lane < tail - HALO * last_edge, part, 0.0)

    wide = lax.broadcasted_iota(jnp.int32, (SUB, LANES), 1)
    row = lax.broadcasted_iota(jnp.int32, (SUB, LANES), 0)
    reach = 4

    def channel(c, local):
        g = g_scr[pl.ds(c, seqs * (blocks + 1), stride=width), :]
        pair = jnp.concatenate([g[: seqs * blocks].astype(BF16), g[seqs:].astype(BF16)], axis=1)
        tap = jnp.broadcast_to(p_scr[pl.ds(c, 1), :], (SUB, LANES))
        tap = jnp.where(wide >= LANES - taps, tap, 0.0)
        first = pltpu.roll(tap, 0, 1, stride=1, stride_axis=0)
        low, high = [], []
        for k in range(LANES // SUB):
            f = first if k == 0 else pltpu.roll(first, SUB * k, 1)
            if k < reach:
                under = wide < row + SUB * k
                low.append(jnp.where(under, f, 0.0))
                high.append(jnp.where(under, 0.0, f))
            else:
                low.append(f)
        zero = jnp.zeros((LANES - reach * SUB, LANES), F32)
        band = jnp.concatenate(low + high + [zero], axis=0).astype(BF16)
        y = jnp.dot(pair, band, preferred_element_type=F32)
        y_scr[pl.ds(local, seqs * blocks, stride=chunk + 1), :] = y
        parts = y.reshape(blocks, seqs, LANES)
        s_scr[pl.ds(c, 1), :] = jnp.sum(jnp.sum(parts, axis=0), axis=0, keepdims=True)
        q_scr[pl.ds(c, 1), :] = jnp.sum(jnp.sum(parts * parts, axis=0), axis=0, keepdims=True)

    unroll = 32

    @pl.loop(0, width // chunk)
    def _(n):
        base = pl.multiple_of(n * chunk, chunk)

        @pl.loop(0, chunk // unroll)
        def _(i):
            for u in range(unroll):
                local = i * unroll + u
                channel(base + local, local)

        for r in range(seqs * blocks):
            lo = r * (chunk + 1)
            y_ref[r, pl.ds(base, chunk), :] = y_scr[lo : lo + chunk, :].astype(BF16)

    total = jnp.sum(s_scr[...].T, axis=0, keepdims=True)
    square = jnp.sum(q_scr[...].T, axis=0, keepdims=True)
    st_ref[...] = jnp.broadcast_to(jnp.concatenate([total, square], axis=0)[None], st_ref.shape)


def back_kernel(count, group, st_ref, pt_ref, y_ref, x_ref, wo_ref, o_hbm, scale_scr, shift_scr, o_scr, sems):
    seqs, frames, width = x_ref.shape
    blocks = frames // LANES
    per = seqs // group
    both = jnp.sum(st_ref[...], axis=0)
    mean = both[0:1] * (1.0 / count)
    var = jnp.maximum(both[1:2] * (1.0 / count) - mean * mean, 0.0)
    scale = pt_ref[C_BN_GAIN : C_BN_GAIN + 1, :] * lax.rsqrt(var + EPSILON)
    shift = pt_ref[C_BN_BIAS : C_BN_BIAS + 1, :] - mean * scale
    scale_scr[...] = jnp.broadcast_to(scale * 0.5, (LANES, width)).T
    shift_scr[...] = jnp.broadcast_to(shift * 0.5, (LANES, width)).T
    out_bias = pt_ref[C_B_OUT : C_B_OUT + 1, :]

    def copy(b, s):
        target = o_hbm.at[s, pl.ds(pl.multiple_of(b * LANES, LANES), LANES), :]
        slot = lax.rem(b, 2)
        return pltpu.make_async_copy(o_scr.at[slot, s], target, sems.at[slot, s])

    @pl.loop(0, blocks)
    def _(b):
        for p in range(per):
            acts = []
            for s in range(p * group, (p + 1) * group):
                half = y_ref[b * seqs + s].astype(F32) * scale_scr[...] + shift_scr[...]
                acts.append((half + half * jnp.tanh(half)).astype(BF16))
            act = jnp.concatenate(acts, axis=1)
            proj = lax.dot_general(act, wo_ref[...], (((0,), (0,)), ((), ())), preferred_element_type=F32)

            @pl.when(b > 1)
            def _():
                for s in range(p * group, (p + 1) * group):
                    copy(b - 2, s).wait()

            at = pl.multiple_of(b * LANES, LANES)
            for q in range(group):
                s = p * group + q
                rest = x_ref[s, pl.ds(at, LANES), :].astype(F32) + out_bias
                o_scr[lax.rem(b, 2), s] = proj[LANES * q : LANES * (q + 1)] + rest
                copy(b, s).start()

    for b in range(max(blocks - 2, 0), blocks):
        for s in range(seqs):
            copy(b, s).wait()


def shards(inputs, ln_gain, ln_bias, w_in, b_in, w_depth, bn_gain, bn_bias, w_out, b_out):
    seqs, frames, width = inputs.shape
    rows, taps = w_depth.shape
    seq_size, batch_size = lax.axis_size("seq"), lax.axis_size("batch")
    devices = seq_size * batch_size
    seq_me, batch_me = lax.axis_index("seq"), lax.axis_index("batch")
    stages = bit_stages(seq_size, batch_size)
    vmem = pl.BlockSpec(memory_space=pltpu.VMEM)
    blocks = frames // LANES

    packed = pl.pallas_call(
        functools.partial(pack_kernel, taps),
        out_shape=jax.ShapeDtypeStruct((rows, 3 * width + LANES), BF16),
        in_specs=[vmem] * 9,
        out_specs=vmem,
        name="pack",
    )(ln_gain, ln_bias, w_in, b_in, w_depth, bn_gain, bn_bias, w_out, b_out)
    ends = seq_size - 1
    left = lax.ppermute(inputs[:, frames - HALO :], "seq", [(i, i + 1) for i in range(ends)])
    right = lax.ppermute(inputs[:, :HALO], "seq", [(i + 1, i) for i in range(ends)])
    flat = gather_relative(packed, stages, 2)

    pieces, at = (seq_size, batch_size), (seq_me, batch_me)
    if rows % 16:
        order = jnp.stack([relative_place(seq_me ^ (d // batch_size), batch_me ^ (d % batch_size), stages) for d in range(devices)])
        flat = jnp.take(jnp.concatenate(flat, axis=0), order, axis=0)
        for start in (2 * width + C_B_IN, 2 * width + LANES // 2 + C_B_IN):
            cut = flat[:, :, start : start + 2].transpose(0, 2, 1).reshape(2, width).T.reshape(devices, rows, 2)
            flat = lax.dynamic_update_slice(flat, cut, (0, 0, start))
        flat = [flat.reshape(1, width, -1)]
        pieces, at, stages = (1, 1), (0 * seq_me, 0 * batch_me), []
    place = jnp.stack([*at, seq_me == 0, seq_me == ends]).astype(jnp.int32)

    chunk = 64
    y, st, wo, pt, x = pl.pallas_call(
        functools.partial(front_kernel, taps, stages, *pieces),
        out_shape=(
            pltpu.VMEM((seqs * blocks, width, LANES), BF16),
            jax.ShapeDtypeStruct((devices, 2, width), F32),
            pltpu.VMEM((width, width), BF16),
            pltpu.VMEM((LANES, width), F32),
            pltpu.VMEM((seqs, frames, width), BF16),
        ),
        in_specs=[pl.BlockSpec(memory_space=pltpu.SMEM)] + [vmem] * len(flat) + [pl.BlockSpec(memory_space=pl.ANY)] + [vmem] * 2,
        out_specs=[vmem] * 5,
        scratch_shapes=[
            pltpu.VMEM((width, 2 * width), F32),
            pltpu.VMEM((2 * width, width), BF16),
            pltpu.VMEM((2 * width, LANES), F32),
            pltpu.VMEM((width, LANES), F32),
            pltpu.VMEM(((blocks + 1) * seqs * width, LANES), F32),
            pltpu.VMEM((seqs * blocks * (chunk + 1), LANES), F32),
            pltpu.VMEM((width, LANES), F32),
            pltpu.VMEM((width, LANES), F32),
            pltpu.SemaphoreType.DMA((seqs,)),
        ],
        compiler_params=pltpu.CompilerParams(vmem_limit_bytes=FRONT_VMEM),
        name="front",
    )(place, *flat, inputs, left, right)

    st = lax.all_to_all(st, ("seq", "batch"), 0, 0)

    group = 8
    y, x, wo, pt = (pltpu.with_memory_space_constraint(a, pltpu.VMEM) for a in (y, x, wo, pt))
    return pl.pallas_call(
        functools.partial(back_kernel, float(seqs * frames * devices), group),
        out_shape=jax.ShapeDtypeStruct((seqs, frames, width), F32),
        in_specs=[vmem] * 5,
        out_specs=pl.BlockSpec(memory_space=pl.ANY),
        scratch_shapes=[
            pltpu.VMEM((width, LANES), F32),
            pltpu.VMEM((width, LANES), F32),
            pltpu.VMEM((2, seqs, LANES, width), F32),
            pltpu.SemaphoreType.DMA((2, seqs)),
        ],
        compiler_params=pltpu.CompilerParams(vmem_limit_bytes=BACK_VMEM),
        name="back",
    )(st, pt, y, x, wo)


def solution(mesh):
    channel = P(("seq", "batch"))
    matrix = P(("seq", "batch"), None)
    return jax.shard_map(
        shards,
        mesh=mesh,
        in_specs=(
            P("batch", "seq", None), channel, channel, matrix, channel, matrix, channel, channel, matrix, channel,
        ),
        out_specs=P("batch", "seq", None),
        check_vma=False,
    )
```

```python
import functools

import jax
import jax.numpy as jnp
from jax import lax
from jax.experimental import pallas as pl
from jax.experimental.pallas import tpu as pltpu
from jax.sharding import PartitionSpec as P

EPSILON = 1e-05
F32 = jnp.float32
BF16 = jnp.bfloat16
HALO = 16
LANES = 128
FRONT_VMEM = 36 * 1024 * 1024
BACK_VMEM = 16 * 1024 * 1024
SUB = 8
C_LN_GAIN, C_LN_BIAS, C_BN_GAIN, C_BN_BIAS, C_B_OUT, C_B_IN = 0, 1, 2, 3, 4, 5


def bit_stages(seq_size, batch_size):
    stages = []
    for axis, size, low in (("batch", batch_size, 0), ("seq", seq_size, 1)):
        at, top = low, size.bit_length() - 1
        while at < top:
            bits = min(2, top - at)
            stages.append((axis, at, bits))
            at += bits
    if seq_size > 1:
        stages.append(("seq", 0, 1))
    return stages


def gather_relative(block, stages, keep):
    lists = [block[None]]
    for index, (axis, shift, bits) in enumerate(stages):
        if index <= len(stages) - keep:
            lists = [lists[0] if len(lists) == 1 else jnp.concatenate(lists, axis=0)]
        size = lax.axis_size(axis)
        parts = list(lists)
        for m in range(1, 1 << bits):
            pairs = [(i, i ^ (m << shift)) for i in range(size)]
            parts += [lax.ppermute(a, axis, pairs) for a in lists]
        lists = parts
    return lists


def relative_place(seq_xor, batch_xor, stages):
    place, weight = 0, 1
    for axis, shift, bits in stages:
        word = seq_xor if axis == "seq" else batch_xor
        digit = (word >> shift) & ((1 << bits) - 1)
        place = place + digit * weight
        weight <<= bits
    return place


def pack_kernel(taps, ln_gain, ln_bias, w_in, b_in, w_depth, bn_gain, bn_bias, w_out, b_out, o_ref):
    rows, small = w_in.shape
    lane = lax.broadcasted_iota(jnp.int32, (rows, LANES), 1)
    row = lax.broadcasted_iota(jnp.int32, (rows, LANES), 0)

    def column(ref, start=0):
        line = jnp.broadcast_to(ref[...].reshape(1, -1), (rows, ref.shape[0]))
        hit = lane[:, : line.shape[1]] == row[:, : line.shape[1]] + start
        return jnp.sum(jnp.where(hit, line, 0.0), axis=1, keepdims=True)

    cells = (
        (C_LN_GAIN, column(ln_gain)),
        (C_LN_BIAS, column(ln_bias)),
        (C_BN_GAIN, column(bn_gain)),
        (C_BN_BIAS, column(bn_bias)),
        (C_B_OUT, column(b_out)),
        (C_B_IN, column(b_in)),
        (C_B_IN + 1, column(b_in, rows)),
    ) + tuple((LANES // 2 - 1 - k, w_depth[:, k : k + 1]) for k in range(taps))
    cell = jnp.zeros((rows, LANES), F32)
    for at, value in cells:
        cell = jnp.where((lane & (LANES // 2 - 1)) == at, value, cell)
    high = cell.astype(BF16)
    low = (cell - high.astype(F32)).astype(BF16)
    o_ref[:, :small] = w_in[...]
    o_ref[:, small : small + LANES] = jnp.where(lane < LANES // 2, high.astype(F32), low.astype(F32)).astype(BF16)
    o_ref[:, small + LANES :] = w_out[...]


def front_kernel(taps, stages, seq_size, batch_size, where_ref, *refs):
    flat_refs, refs = refs[:-17], refs[-17:]
    front_body(taps, stages, seq_size, batch_size, where_ref, flat_refs, *refs)


def front_body(taps, stages, seq_size, batch_size, where_ref, flat_refs, x_hbm, left_ref, right_ref,
                 y_ref, st_ref, wo_ref, pt_ref, x_ref,
                 w_scr, wt_scr, bb_scr, p_scr, g_scr, y_scr, s_scr, q_scr, sems):
    seqs, frames, width = x_ref.shape
    blocks = frames // LANES
    chunk = y_scr.shape[0] // (seqs * blocks) - 1
    small = 2 * width
    rows = width // (seq_size * batch_size)
    seq_me, batch_me = where_ref[0], where_ref[1]
    first_edge, last_edge = where_ref[2], where_ref[3]

    loads = [pltpu.make_async_copy(x_hbm.at[s], x_ref.at[s], sems.at[s]) for s in range(seqs)]
    for load in loads:
        load.start()

    for s in range(seq_size):
        for b in range(batch_size):
            at = relative_place(s, b, stages)
            flat_ref, at = flat_refs[at // flat_refs[0].shape[0]], at % flat_refs[0].shape[0]
            lo = pl.multiple_of(((seq_me ^ s) * batch_size + (batch_me ^ b)) * rows, rows)
            w_scr[pl.ds(lo, rows), :] = flat_ref[at, :, 0:small].astype(F32) * 0.5
            wo_ref[pl.ds(lo, rows), :] = flat_ref[at, :, small + LANES :]
            cell = flat_ref[at, :, small : small + LANES].astype(F32)
            cell = cell + pltpu.roll(cell, LANES // 2, 1)
            p_scr[pl.ds(lo, rows), :] = cell
            for h in range(2):
                col = cell[:, C_B_IN + h : C_B_IN + h + 1] * 0.5
                bb_scr[pl.ds(pl.multiple_of(2 * lo + h * rows, rows), rows), :] = jnp.broadcast_to(col, (rows, LANES))
    for j in range(0, small, 256):
        wt_scr[j : j + 256, :] = w_scr[:, j : j + 256].T.astype(BF16)
    pt_ref[...] = p_scr[...].T
    for load in loads:
        load.wait()

    gain = pt_ref[C_LN_GAIN : C_LN_GAIN + 1, :]
    bias = pt_ref[C_LN_BIAS : C_LN_BIAS + 1, :]

    def normed(part):
        part = part.astype(F32)
        centre = jnp.mean(part, axis=-1, keepdims=True)
        part = part - centre
        spread = jnp.mean(part * part, axis=-1, keepdims=True)
        return (part * lax.rsqrt(spread + EPSILON) * gain + bias).astype(BF16)

    def gated(part):
        hid = lax.dot_general(wt_scr[...], part, (((1,), (1,)), ((), ())), preferred_element_type=F32)
        add = jnp.concatenate([bb_scr[...]] * (hid.shape[1] // LANES), axis=1)
        hid = hid + add
        val = hid[:width]
        return val + val * jnp.tanh(hid[width:])

    lane = lax.broadcasted_iota(jnp.int32, (1, LANES), 1)

    def block(b, piece, edge):
        for s in range(0, seqs, 2):
            glu = gated(normed(jnp.concatenate([piece(s), piece(s + 1)], axis=0)))
            for h in range(2):
                part = glu[:, h * LANES : (h + 1) * LANES]
                if edge is not None:
                    part = jnp.where(lane >= edge, part, 0.0)
                to = b * seqs * (width + 1)
                to = to if isinstance(b, int) else pl.multiple_of(to, SUB)
                g_scr[pl.ds(to + (s + h) * (width + 1), width), :] = part

    block(0, lambda s: jnp.concatenate([left_ref[s], x_ref[s, : LANES - HALO, :]], axis=0), HALO * first_edge)

    @pl.loop(1, blocks)
    def _(b):
        at = pl.multiple_of(b * LANES - HALO, HALO)
        block(b, lambda s: x_ref[s, pl.ds(at, LANES), :], None)

    tail = 2 * HALO
    ends = []
    for s in range(seqs):
        ends += [x_ref[s, frames - HALO :, :], right_ref[s]]
    glu = gated(normed(jnp.concatenate(ends, axis=0)))
    per = LANES // tail
    for s in range(seqs):
        part = glu[:, (s // per) * LANES : (s // per + 1) * LANES]
        move = (s % per) * tail
        if move:
            part = pltpu.roll(part, LANES - move, 1)
        to = (blocks * seqs + s) * (width + 1)
        g_scr[to : to + width, :] = jnp.where(lane < tail - HALO * last_edge, part, 0.0)

    wide = lax.broadcasted_iota(jnp.int32, (SUB, LANES), 1)
    row = lax.broadcasted_iota(jnp.int32, (SUB, LANES), 0)
    reach = 4

    def channel(c, local):
        g = g_scr[pl.ds(c, seqs * (blocks + 1), stride=width + 1), :]
        pair = jnp.concatenate([g[: seqs * blocks].astype(BF16), g[seqs:].astype(BF16)], axis=1)
        tap = jnp.broadcast_to(p_scr[pl.ds(c, 1), :], (SUB, LANES))
        tap = jnp.where(wide >= LANES - taps, tap, 0.0)
        first = pltpu.roll(tap, 0, 1, stride=1, stride_axis=0)
        low, high = [], []
        for k in range(LANES // SUB):
            f = first if k == 0 else pltpu.roll(first, SUB * k, 1)
            if k < reach:
                under = wide < row + SUB * k
                low.append(jnp.where(under, f, 0.0))
                high.append(jnp.where(under, 0.0, f))
            else:
                low.append(f)
        zero = jnp.zeros((LANES - reach * SUB, LANES), F32)
        band = jnp.concatenate(low + high + [zero], axis=0).astype(BF16)
        y = jnp.dot(pair, band, preferred_element_type=F32)
        y_scr[pl.ds(local, seqs * blocks, stride=chunk + 1), :] = y
        parts = y.reshape(blocks, seqs, LANES)
        s_scr[pl.ds(c, 1), :] = jnp.sum(jnp.sum(parts, axis=0), axis=0, keepdims=True)
        q_scr[pl.ds(c, 1), :] = jnp.sum(jnp.sum(parts * parts, axis=0), axis=0, keepdims=True)

    unroll = 32

    @pl.loop(0, width // chunk)
    def _(n):
        base = pl.multiple_of(n * chunk, chunk)

        @pl.loop(0, chunk // unroll)
        def _(i):
            for u in range(unroll):
                local = i * unroll + u
                channel(base + local, local)

        for r in range(seqs * blocks):
            lo = r * (chunk + 1)
            y_ref[r, pl.ds(base, chunk), :] = y_scr[lo : lo + chunk, :].astype(BF16)

    total = jnp.sum(s_scr[...].T, axis=0, keepdims=True)
    square = jnp.sum(q_scr[...].T, axis=0, keepdims=True)
    st_ref[...] = jnp.broadcast_to(jnp.concatenate([total, square], axis=0)[None], st_ref.shape)


def back_kernel(count, group, st_ref, pt_ref, y_ref, x_ref, wo_ref, o_hbm, scale_scr, shift_scr, o_scr, sems):
    seqs, frames, width = x_ref.shape
    blocks = frames // LANES
    per = seqs // group
    both = jnp.sum(st_ref[...], axis=0)
    mean = both[0:1] * (1.0 / count)
    var = jnp.maximum(both[1:2] * (1.0 / count) - mean * mean, 0.0)
    scale = pt_ref[C_BN_GAIN : C_BN_GAIN + 1, :] * lax.rsqrt(var + EPSILON)
    shift = pt_ref[C_BN_BIAS : C_BN_BIAS + 1, :] - mean * scale
    scale_scr[...] = jnp.broadcast_to(scale * 0.5, (LANES, width)).T
    shift_scr[...] = jnp.broadcast_to(shift * 0.5, (LANES, width)).T
    out_bias = pt_ref[C_B_OUT : C_B_OUT + 1, :]

    def copy(b, s):
        target = o_hbm.at[s, pl.ds(pl.multiple_of(b * LANES, LANES), LANES), :]
        slot = lax.rem(b, 2)
        return pltpu.make_async_copy(o_scr.at[slot, s], target, sems.at[slot, s])

    @pl.loop(0, blocks)
    def _(b):
        for p in range(per):
            acts = []
            for s in range(p * group, (p + 1) * group):
                half = y_ref[b * seqs + s].astype(F32) * scale_scr[...] + shift_scr[...]
                acts.append((half + half * jnp.tanh(half)).astype(BF16))
            act = jnp.concatenate(acts, axis=1)
            proj = lax.dot_general(act, wo_ref[...], (((0,), (0,)), ((), ())), preferred_element_type=F32)

            @pl.when(b > 1)
            def _():
                for s in range(p * group, (p + 1) * group):
                    copy(b - 2, s).wait()

            at = pl.multiple_of(b * LANES, LANES)
            for q in range(group):
                s = p * group + q
                rest = x_ref[s, pl.ds(at, LANES), :].astype(F32) + out_bias
                o_scr[lax.rem(b, 2), s] = proj[LANES * q : LANES * (q + 1)] + rest
                copy(b, s).start()

    for b in range(max(blocks - 2, 0), blocks):
        for s in range(seqs):
            copy(b, s).wait()


def shards(inputs, ln_gain, ln_bias, w_in, b_in, w_depth, bn_gain, bn_bias, w_out, b_out):
    seqs, frames, width = inputs.shape
    rows, taps = w_depth.shape
    seq_size, batch_size = lax.axis_size("seq"), lax.axis_size("batch")
    devices = seq_size * batch_size
    seq_me, batch_me = lax.axis_index("seq"), lax.axis_index("batch")
    stages = bit_stages(seq_size, batch_size)
    vmem = pl.BlockSpec(memory_space=pltpu.VMEM)
    blocks = frames // LANES

    packed = pl.pallas_call(
        functools.partial(pack_kernel, taps),
        out_shape=jax.ShapeDtypeStruct((rows, 3 * width + LANES), BF16),
        in_specs=[vmem] * 9,
        out_specs=vmem,
        name="pack",
    )(ln_gain, ln_bias, w_in, b_in, w_depth, bn_gain, bn_bias, w_out, b_out)
    ends = seq_size - 1
    left = lax.ppermute(inputs[:, frames - HALO :], "seq", [(i, i + 1) for i in range(ends)])
    right = lax.ppermute(inputs[:, :HALO], "seq", [(i + 1, i) for i in range(ends)])
    flat = gather_relative(packed, stages, 2)

    pieces, at = (seq_size, batch_size), (seq_me, batch_me)
    if rows % 16:
        order = jnp.stack([relative_place(seq_me ^ (d // batch_size), batch_me ^ (d % batch_size), stages) for d in range(devices)])
        flat = jnp.take(jnp.concatenate(flat, axis=0), order, axis=0)
        for start in (2 * width + C_B_IN, 2 * width + LANES // 2 + C_B_IN):
            cut = flat[:, :, start : start + 2].transpose(0, 2, 1).reshape(2, width).T.reshape(devices, rows, 2)
            flat = lax.dynamic_update_slice(flat, cut, (0, 0, start))
        flat = [flat.reshape(1, width, -1)]
        pieces, at, stages = (1, 1), (0 * seq_me, 0 * batch_me), []
    place = jnp.stack([*at, seq_me == 0, seq_me == ends]).astype(jnp.int32)

    chunk = 64
    y, st, wo, pt, x = pl.pallas_call(
        functools.partial(front_kernel, taps, stages, *pieces),
        out_shape=(
            pltpu.VMEM((seqs * blocks, width, LANES), BF16),
            jax.ShapeDtypeStruct((devices, 2, width), F32),
            pltpu.VMEM((width, width), BF16),
            pltpu.VMEM((LANES, width), F32),
            pltpu.VMEM((seqs, frames, width), BF16),
        ),
        in_specs=[pl.BlockSpec(memory_space=pltpu.SMEM)] + [vmem] * len(flat) + [pl.BlockSpec(memory_space=pl.ANY)] + [vmem] * 2,
        out_specs=[vmem] * 5,
        scratch_shapes=[
            pltpu.VMEM((width, 2 * width), F32),
            pltpu.VMEM((2 * width, width), BF16),
            pltpu.VMEM((2 * width, LANES), F32),
            pltpu.VMEM((width, LANES), F32),
            pltpu.VMEM(((blocks + 1) * seqs * (width + 1), LANES), F32),
            pltpu.VMEM((seqs * blocks * (chunk + 1), LANES), F32),
            pltpu.VMEM((width, LANES), F32),
            pltpu.VMEM((width, LANES), F32),
            pltpu.SemaphoreType.DMA((seqs,)),
        ],
        compiler_params=pltpu.CompilerParams(vmem_limit_bytes=FRONT_VMEM),
        name="front",
    )(place, *flat, inputs, left, right)

    st = lax.all_to_all(st, ("seq", "batch"), 0, 0)

    group = 8
    y, x, wo, pt = (pltpu.with_memory_space_constraint(a, pltpu.VMEM) for a in (y, x, wo, pt))
    return pl.pallas_call(
        functools.partial(back_kernel, float(seqs * frames * devices), group),
        out_shape=jax.ShapeDtypeStruct((seqs, frames, width), F32),
        in_specs=[vmem] * 5,
        out_specs=pl.BlockSpec(memory_space=pl.ANY),
        scratch_shapes=[
            pltpu.VMEM((width, LANES), F32),
            pltpu.VMEM((width, LANES), F32),
            pltpu.VMEM((2, seqs, LANES, width), F32),
            pltpu.SemaphoreType.DMA((2, seqs)),
        ],
        compiler_params=pltpu.CompilerParams(vmem_limit_bytes=BACK_VMEM),
        name="back",
    )(st, pt, y, x, wo)


def solution(mesh):
    channel = P(("seq", "batch"))
    matrix = P(("seq", "batch"), None)
    return jax.shard_map(
        shards,
        mesh=mesh,
        in_specs=(
            P("batch", "seq", None), channel, channel, matrix, channel, matrix, channel, channel, matrix, channel,
        ),
        out_specs=P("batch", "seq", None),
        check_vma=False,
    )
```

```python
import functools

import jax
import jax.numpy as jnp
from jax import lax
from jax.experimental import pallas as pl
from jax.experimental.pallas import tpu as pltpu
from jax.sharding import PartitionSpec as P

EPSILON = 1e-05
F32 = jnp.float32
BF16 = jnp.bfloat16
HALO = 16
LANES = 128
FRONT_VMEM = 36 * 1024 * 1024
BACK_VMEM = 16 * 1024 * 1024
SUB = 8
C_LN_GAIN, C_LN_BIAS, C_BN_GAIN, C_BN_BIAS, C_B_OUT, C_B_IN = 0, 1, 2, 3, 4, 5


def bit_stages(seq_size, batch_size):
    stages = []
    for axis, size, low in (("batch", batch_size, 0), ("seq", seq_size, 1)):
        at, top = low, size.bit_length() - 1
        while at < top:
            bits = min(2, top - at)
            stages.append((axis, at, bits))
            at += bits
    if seq_size > 1:
        stages.append(("seq", 0, 1))
    return stages


def gather_relative(block, stages, keep):
    lists = [block[None]]
    for index, (axis, shift, bits) in enumerate(stages):
        if index <= len(stages) - keep:
            lists = [lists[0] if len(lists) == 1 else jnp.concatenate(lists, axis=0)]
        size = lax.axis_size(axis)
        parts = list(lists)
        for m in range(1, 1 << bits):
            pairs = [(i, i ^ (m << shift)) for i in range(size)]
            parts += [lax.ppermute(a, axis, pairs) for a in lists]
        lists = parts
    return lists


def relative_place(seq_xor, batch_xor, stages):
    place, weight = 0, 1
    for axis, shift, bits in stages:
        word = seq_xor if axis == "seq" else batch_xor
        digit = (word >> shift) & ((1 << bits) - 1)
        place = place + digit * weight
        weight <<= bits
    return place


def pack_kernel(taps, ln_gain, ln_bias, w_in, b_in, w_depth, bn_gain, bn_bias, w_out, b_out, o_ref):
    rows, small = w_in.shape
    lane = lax.broadcasted_iota(jnp.int32, (rows, LANES), 1)
    row = lax.broadcasted_iota(jnp.int32, (rows, LANES), 0)

    def column(ref, start=0):
        line = jnp.broadcast_to(ref[...].reshape(1, -1), (rows, ref.shape[0]))
        hit = lane[:, : line.shape[1]] == row[:, : line.shape[1]] + start
        return jnp.sum(jnp.where(hit, line, 0.0), axis=1, keepdims=True)

    cells = (
        (C_LN_GAIN, column(ln_gain)),
        (C_LN_BIAS, column(ln_bias)),
        (C_BN_GAIN, column(bn_gain)),
        (C_BN_BIAS, column(bn_bias)),
        (C_B_OUT, column(b_out)),
        (C_B_IN, column(b_in)),
        (C_B_IN + 1, column(b_in, rows)),
    ) + tuple((LANES // 2 - 1 - k, w_depth[:, k : k + 1]) for k in range(taps))
    cell = jnp.zeros((rows, LANES), F32)
    for at, value in cells:
        cell = jnp.where((lane & (LANES // 2 - 1)) == at, value, cell)
    high = cell.astype(BF16)
    low = (cell - high.astype(F32)).astype(BF16)
    o_ref[:, :small] = w_in[...]
    o_ref[:, small : small + LANES] = jnp.where(lane < LANES // 2, high.astype(F32), low.astype(F32)).astype(BF16)
    o_ref[:, small + LANES :] = w_out[...]


def front_kernel(taps, stages, seq_size, batch_size, where_ref, *refs):
    flat_refs, refs = refs[:-17], refs[-17:]
    front_body(taps, stages, seq_size, batch_size, where_ref, flat_refs, *refs)


def front_body(taps, stages, seq_size, batch_size, where_ref, flat_refs, x_hbm, left_ref, right_ref,
                 y_ref, st_ref, wo_ref, pt_ref, x_ref,
                 w_scr, wt_scr, bb_scr, p_scr, g_scr, y_scr, s_scr, q_scr, sems):
    seqs, frames, width = x_ref.shape
    blocks = frames // LANES
    chunk = y_scr.shape[0] // (seqs * blocks) - 1
    small = 2 * width
    rows = width // (seq_size * batch_size)
    seq_me, batch_me = where_ref[0], where_ref[1]
    first_edge, last_edge = where_ref[2], where_ref[3]

    loads = [pltpu.make_async_copy(x_hbm.at[s], x_ref.at[s], sems.at[s]) for s in range(seqs)]
    for load in loads:
        load.start()

    for s in range(seq_size):
        for b in range(batch_size):
            at = relative_place(s, b, stages)
            flat_ref, at = flat_refs[at // flat_refs[0].shape[0]], at % flat_refs[0].shape[0]
            lo = pl.multiple_of(((seq_me ^ s) * batch_size + (batch_me ^ b)) * rows, rows)
            w_scr[pl.ds(lo, rows), :] = flat_ref[at, :, 0:small].astype(F32) * 0.5
            wo_ref[pl.ds(lo, rows), :] = flat_ref[at, :, small + LANES :]
            cell = flat_ref[at, :, small : small + LANES].astype(F32)
            cell = cell + pltpu.roll(cell, LANES // 2, 1)
            p_scr[pl.ds(lo, rows), :] = cell
            for h in range(2):
                col = cell[:, C_B_IN + h : C_B_IN + h + 1] * 0.5
                bb_scr[pl.ds(pl.multiple_of(2 * lo + h * rows, rows), rows), :] = jnp.broadcast_to(col, (rows, LANES))
    for j in range(0, small, 256):
        wt_scr[j : j + 256, :] = w_scr[:, j : j + 256].T.astype(BF16)
    pt_ref[...] = p_scr[...].T

    gain = pt_ref[C_LN_GAIN : C_LN_GAIN + 1, :]
    bias = pt_ref[C_LN_BIAS : C_LN_BIAS + 1, :]

    def normed(part):
        part = part.astype(F32)
        centre = jnp.mean(part, axis=-1, keepdims=True)
        part = part - centre
        spread = jnp.mean(part * part, axis=-1, keepdims=True)
        return (part * lax.rsqrt(spread + EPSILON) * gain + bias).astype(BF16)

    def gated(part):
        hid = lax.dot_general(wt_scr[...], part, (((1,), (1,)), ((), ())), preferred_element_type=F32)
        add = jnp.concatenate([bb_scr[...]] * (hid.shape[1] // LANES), axis=1)
        hid = hid + add
        val = hid[:width]
        return val + val * jnp.tanh(hid[width:])

    lane = lax.broadcasted_iota(jnp.int32, (1, LANES), 1)

    def block(b, piece, edge):
        for s in range(0, seqs, 2):
            glu = gated(normed(jnp.concatenate([piece(s), piece(s + 1)], axis=0)))
            for h in range(2):
                part = glu[:, h * LANES : (h + 1) * LANES]
                if edge is not None:
                    part = jnp.where(lane >= edge, part, 0.0)
                to = b * seqs * (width + 1)
                to = to if isinstance(b, int) else pl.multiple_of(to, SUB)
                g_scr[pl.ds(to + (s + h) * (width + 1), width), :] = part

    def start_piece(s):
        loads[s].wait()
        return jnp.concatenate([left_ref[s], x_ref[s, : LANES - HALO, :]], axis=0)

    block(0, start_piece, HALO * first_edge)

    @pl.loop(1, blocks)
    def _(b):
        at = pl.multiple_of(b * LANES - HALO, HALO)
        block(b, lambda s: x_ref[s, pl.ds(at, LANES), :], None)

    tail = 2 * HALO
    ends = []
    for s in range(seqs):
        ends += [x_ref[s, frames - HALO :, :], right_ref[s]]
    glu = gated(normed(jnp.concatenate(ends, axis=0)))
    per = LANES // tail
    for s in range(seqs):
        part = glu[:, (s // per) * LANES : (s // per + 1) * LANES]
        move = (s % per) * tail
        if move:
            part = pltpu.roll(part, LANES - move, 1)
        to = (blocks * seqs + s) * (width + 1)
        g_scr[to : to + width, :] = jnp.where(lane < tail - HALO * last_edge, part, 0.0)

    wide = lax.broadcasted_iota(jnp.int32, (SUB, LANES), 1)
    row = lax.broadcasted_iota(jnp.int32, (SUB, LANES), 0)
    reach = 4

    def channel(c, local):
        g = g_scr[pl.ds(c, seqs * (blocks + 1), stride=width + 1), :]
        pair = jnp.concatenate([g[: seqs * blocks].astype(BF16), g[seqs:, : reach * SUB].astype(BF16)], axis=1)
        tap = jnp.broadcast_to(p_scr[pl.ds(c, 1), :], (SUB, LANES))
        tap = jnp.where(wide >= LANES - taps, tap, 0.0)
        first = pltpu.roll(tap, 0, 1, stride=1, stride_axis=0)
        low, high = [], []
        for k in range(LANES // SUB):
            f = first if k == 0 else pltpu.roll(first, SUB * k, 1)
            if k < reach:
                under = wide < row + SUB * k
                low.append(jnp.where(under, f, 0.0))
                high.append(jnp.where(under, 0.0, f))
            else:
                low.append(f)
        band = jnp.concatenate(low + high, axis=0).astype(BF16)
        y = jnp.dot(pair, band, preferred_element_type=F32)
        y_scr[pl.ds(local, seqs * blocks, stride=chunk + 1), :] = y
        parts = y.reshape(blocks, seqs, LANES)
        s_scr[pl.ds(c, 1), :] = jnp.sum(jnp.sum(parts, axis=0), axis=0, keepdims=True)
        q_scr[pl.ds(c, 1), :] = jnp.sum(jnp.sum(parts * parts, axis=0), axis=0, keepdims=True)

    unroll = 32

    @pl.loop(0, width // chunk)
    def _(n):
        base = pl.multiple_of(n * chunk, chunk)

        @pl.loop(0, chunk // unroll)
        def _(i):
            for u in range(unroll):
                local = i * unroll + u
                channel(base + local, local)

        for r in range(seqs * blocks):
            lo = r * (chunk + 1)
            y_ref[r, pl.ds(base, chunk), :] = y_scr[lo : lo + chunk, :].astype(BF16)

    total = jnp.sum(s_scr[...].T, axis=0, keepdims=True)
    square = jnp.sum(q_scr[...].T, axis=0, keepdims=True)
    st_ref[...] = jnp.broadcast_to(jnp.concatenate([total, square], axis=0)[None], st_ref.shape)


def back_kernel(count, group, st_ref, pt_ref, y_ref, x_ref, wo_ref, o_hbm, scale_scr, shift_scr, o_scr, sems):
    seqs, frames, width = x_ref.shape
    blocks = frames // LANES
    per = seqs // group
    both = jnp.sum(st_ref[...], axis=0)
    mean = both[0:1] * (1.0 / count)
    var = jnp.maximum(both[1:2] * (1.0 / count) - mean * mean, 0.0)
    scale = pt_ref[C_BN_GAIN : C_BN_GAIN + 1, :] * lax.rsqrt(var + EPSILON)
    shift = pt_ref[C_BN_BIAS : C_BN_BIAS + 1, :] - mean * scale
    scale_scr[...] = jnp.broadcast_to(scale * 0.5, (LANES, width)).T
    shift_scr[...] = jnp.broadcast_to(shift * 0.5, (LANES, width)).T
    out_bias = pt_ref[C_B_OUT : C_B_OUT + 1, :]

    def copy(b, s):
        target = o_hbm.at[s, pl.ds(pl.multiple_of(b * LANES, LANES), LANES), :]
        slot = lax.rem(b, 2)
        return pltpu.make_async_copy(o_scr.at[slot, s], target, sems.at[slot, s])

    @pl.loop(0, blocks)
    def _(b):
        for p in range(per):
            acts = []
            for s in range(p * group, (p + 1) * group):
                half = y_ref[b * seqs + s].astype(F32) * scale_scr[...] + shift_scr[...]
                acts.append((half + half * jnp.tanh(half)).astype(BF16))
            act = jnp.concatenate(acts, axis=1)
            proj = lax.dot_general(act, wo_ref[...], (((0,), (0,)), ((), ())), preferred_element_type=F32)

            @pl.when(b > 1)
            def _():
                for s in range(p * group, (p + 1) * group):
                    copy(b - 2, s).wait()

            at = pl.multiple_of(b * LANES, LANES)
            for q in range(group):
                s = p * group + q
                rest = x_ref[s, pl.ds(at, LANES), :].astype(F32) + out_bias
                o_scr[lax.rem(b, 2), s] = proj[LANES * q : LANES * (q + 1)] + rest
                copy(b, s).start()

    for b in range(max(blocks - 2, 0), blocks):
        for s in range(seqs):
            copy(b, s).wait()


def shards(inputs, ln_gain, ln_bias, w_in, b_in, w_depth, bn_gain, bn_bias, w_out, b_out):
    seqs, frames, width = inputs.shape
    rows, taps = w_depth.shape
    seq_size, batch_size = lax.axis_size("seq"), lax.axis_size("batch")
    devices = seq_size * batch_size
    seq_me, batch_me = lax.axis_index("seq"), lax.axis_index("batch")
    stages = bit_stages(seq_size, batch_size)
    vmem = pl.BlockSpec(memory_space=pltpu.VMEM)
    blocks = frames // LANES

    packed = pl.pallas_call(
        functools.partial(pack_kernel, taps),
        out_shape=jax.ShapeDtypeStruct((rows, 3 * width + LANES), BF16),
        in_specs=[vmem] * 9,
        out_specs=vmem,
        name="pack",
    )(ln_gain, ln_bias, w_in, b_in, w_depth, bn_gain, bn_bias, w_out, b_out)
    ends = seq_size - 1
    left = lax.ppermute(inputs[:, frames - HALO :], "seq", [(i, i + 1) for i in range(ends)])
    right = lax.ppermute(inputs[:, :HALO], "seq", [(i + 1, i) for i in range(ends)])
    flat = gather_relative(packed, stages, 2)

    pieces, at = (seq_size, batch_size), (seq_me, batch_me)
    if rows % 16:
        order = jnp.stack([relative_place(seq_me ^ (d // batch_size), batch_me ^ (d % batch_size), stages) for d in range(devices)])
        flat = jnp.take(jnp.concatenate(flat, axis=0), order, axis=0)
        for start in (2 * width + C_B_IN, 2 * width + LANES // 2 + C_B_IN):
            cut = flat[:, :, start : start + 2].transpose(0, 2, 1).reshape(2, width).T.reshape(devices, rows, 2)
            flat = lax.dynamic_update_slice(flat, cut, (0, 0, start))
        flat = [flat.reshape(1, width, -1)]
        pieces, at, stages = (1, 1), (0 * seq_me, 0 * batch_me), []
    place = jnp.stack([*at, seq_me == 0, seq_me == ends]).astype(jnp.int32)

    chunk = 64
    y, st, wo, pt, x = pl.pallas_call(
        functools.partial(front_kernel, taps, stages, *pieces),
        out_shape=(
            pltpu.VMEM((seqs * blocks, width, LANES), BF16),
            jax.ShapeDtypeStruct((devices, 2, width), F32),
            pltpu.VMEM((width, width), BF16),
            pltpu.VMEM((LANES, width), F32),
            pltpu.VMEM((seqs, frames, width), BF16),
        ),
        in_specs=[pl.BlockSpec(memory_space=pltpu.SMEM)] + [vmem] * len(flat) + [pl.BlockSpec(memory_space=pl.ANY)] + [vmem] * 2,
        out_specs=[vmem] * 5,
        scratch_shapes=[
            pltpu.VMEM((width, 2 * width), F32),
            pltpu.VMEM((2 * width, width), BF16),
            pltpu.VMEM((2 * width, LANES), F32),
            pltpu.VMEM((width, LANES), F32),
            pltpu.VMEM(((blocks + 1) * seqs * (width + 1), LANES), F32),
            pltpu.VMEM((seqs * blocks * (chunk + 1), LANES), F32),
            pltpu.VMEM((width, LANES), F32),
            pltpu.VMEM((width, LANES), F32),
            pltpu.SemaphoreType.DMA((seqs,)),
        ],
        compiler_params=pltpu.CompilerParams(vmem_limit_bytes=FRONT_VMEM),
        name="front",
    )(place, *flat, inputs, left, right)

    st = lax.all_to_all(st, ("seq", "batch"), 0, 0)

    group = 8
    y, x, wo, pt = (pltpu.with_memory_space_constraint(a, pltpu.VMEM) for a in (y, x, wo, pt))
    return pl.pallas_call(
        functools.partial(back_kernel, float(seqs * frames * devices), group),
        out_shape=jax.ShapeDtypeStruct((seqs, frames, width), F32),
        in_specs=[vmem] * 5,
        out_specs=pl.BlockSpec(memory_space=pl.ANY),
        scratch_shapes=[
            pltpu.VMEM((width, LANES), F32),
            pltpu.VMEM((width, LANES), F32),
            pltpu.VMEM((2, seqs, LANES, width), F32),
            pltpu.SemaphoreType.DMA((2, seqs)),
        ],
        compiler_params=pltpu.CompilerParams(vmem_limit_bytes=BACK_VMEM),
        name="back",
    )(st, pt, y, x, wo)


def solution(mesh):
    channel = P(("seq", "batch"))
    matrix = P(("seq", "batch"), None)
    return jax.shard_map(
        shards,
        mesh=mesh,
        in_specs=(
            P("batch", "seq", None), channel, channel, matrix, channel, matrix, channel, channel, matrix, channel,
        ),
        out_specs=P("batch", "seq", None),
        check_vma=False,
    )
```
